32 devices in a mesh: grp: 4 (over y, core), seq: 8 (over z, x).
Axes of the slice: x: 2, y: 2, z: 4, core: 2. Of those that a mesh axis runs over, the one named last changes fastest.
Arguments:
- query: bfloat16 [16384, 1024], P(('grp', 'seq')), may hold values from -6 to 6
- key_in: bfloat16 [16384, 1024], P(('grp', 'seq')), may hold values from -6 to 6
- value: bfloat16 [16384, 1024], P(('grp', 'seq')), may hold values from -6 to 6
- gate: bfloat16 [16384, 1024], P(('grp', 'seq')), may hold values from -6 to 6
- gain: float32 [1024], replicated, may hold values from 0.1 to 1.9
Outputs:
- attended: bfloat16 [16384, 1024], P(('grp', 'seq'))
The draws below stay inside these ranges and needn't reach their ends.
All inputs are finite; a program needn't handle non-finite values.
Results may differ from the reference program's by a relative error of at most 0.0046.
Values sent between devices are 32-bit elements; how exact they have to be, the bound alone decides.
A program may use at most 320 MiB of HBM per device.

```python
import jax
import jax.numpy as jnp
from jax import lax

HEADS = 8
HEAD_DIM = 128
BLOCK = 256
TOKENS = 16384
FEATURES = 1024


def levels(own_key, dims, cuts, low, top_value):
    factor_of = 1.0
    for axis_at, blocks in cuts:
        heights = jax.random.uniform(jax.random.fold_in(jax.random.fold_in(own_key, 6), axis_at), (blocks,), jnp.float32, low / len(cuts), top_value / len(cuts))
        factor_of = factor_of * jnp.repeat(jnp.exp(heights), dims[axis_at] // blocks).reshape((-1,) + (1,) * (len(dims) - 1 - axis_at))
    return factor_of


def normal_values(rng, dims, scale, most, cuts=(), dtype=jnp.bfloat16):
    drawn = scale * jax.random.normal(rng, dims, jnp.float32)
    if cuts:
        drawn = drawn * levels(rng, dims, cuts, -0.22, 0.18)
    return jnp.clip(drawn, -most, most).astype(dtype)


def setup_inputs(seed: int = 0) -> dict:
    splits = jax.random.split(jax.random.key(seed), 6)
    return {
        "query": normal_values(splits[0], (TOKENS, FEATURES), 1.0, 6.0, ((0, 32),)),
        "key_in": normal_values(splits[1], (TOKENS, FEATURES), 1.0, 6.0, ((0, 32),)),
        "value": normal_values(splits[2], (TOKENS, FEATURES), 1.0, 6.0, ((0, 32),)),
        "gate": normal_values(splits[3], (TOKENS, FEATURES), 1.5, 6.0, ((0, 32),)),
        "gain": jnp.clip(1.0 + 0.18 * jax.random.normal(splits[4], (FEATURES,), jnp.float32), 0.1, 1.9),
    }


def reference(query, key_in, value, gate, gain):
    total_rows = query.shape[0]
    count = total_rows // BLOCK
    queries = jax.nn.silu(query.astype(jnp.float32)).astype(jnp.bfloat16)
    keys_act = jax.nn.silu(key_in.astype(jnp.float32)).astype(jnp.bfloat16)
    queries = queries.reshape(count, BLOCK, HEADS, HEAD_DIM)
    keys_act = keys_act.reshape(count, BLOCK, HEADS, HEAD_DIM)
    values_in = value.reshape(count, BLOCK, HEADS, HEAD_DIM)
    causal = jnp.arange(BLOCK)[:, None] >= jnp.arange(BLOCK)[None, :]

    def advance(state, block_in):
        q_part, k_part, v_part = block_in
        q_wide = q_part.astype(jnp.float32)
        k_wide = k_part.astype(jnp.float32)
        v_wide = v_part.astype(jnp.float32)
        scores = jnp.einsum('thd,shd->hts', q_wide, k_wide)
        scores = jnp.where(causal[None], scores, 0.0).astype(jnp.bfloat16)
        inner = jnp.einsum('hts,shd->thd', scores.astype(jnp.float32), v_wide)
        outer = jnp.einsum('thd,hde->the', q_wide, state, precision=lax.Precision.HIGHEST)
        block_kv = jnp.einsum('thd,the->hde', k_wide, v_wide)
        return (state + block_kv, inner + outer)
    start = jnp.zeros((HEADS, HEAD_DIM, HEAD_DIM), jnp.float32)
    final_state, mixed = lax.scan(advance, start, (queries, keys_act, values_in))
    mixed = mixed.reshape(total_rows, HEADS, HEAD_DIM)
    power = lax.optimization_barrier(jnp.mean(mixed * mixed, axis=-1, keepdims=True))
    normed = (mixed / jnp.sqrt(power + 1e-05)).reshape(total_rows, HEADS * HEAD_DIM)
    result = normed * gain[None, :] * jax.nn.sigmoid(gate.astype(jnp.float32))
    return result.astype(jnp.bfloat16)
```

```python
import functools

import jax
import jax.numpy as jnp
from jax import lax
from jax.experimental import pallas as pl
from jax.experimental.pallas import tpu as pltpu
from jax.sharding import PartitionSpec as P

HEADS = 8
HEAD_DIM = 128
BLOCK = 256
MESH = pl.DeviceIdType.MESH
F32 = jnp.float32
BF16 = jnp.bfloat16


def silu(u):
    u = u.astype(F32)
    return (u / (1.0 + jnp.exp(-u))).astype(BF16)


def kernel(m, n, q_ref, k_ref, v_ref, gate_ref, gain_ref, out_ref, ks, qs, own, first, gather, bases, total,
           state, inner, send1, recv1, send2, recv2, send3, recv3):
    g = lax.axis_index("grp")
    me = lax.axis_index("seq")
    rows = q_ref.shape[0]
    count = rows // BLOCK
    piece = HEADS * HEAD_DIM // n
    per_head = n // HEADS

    def rows_of(j):
        return pl.ds(pl.multiple_of(j * piece, piece), piece)

    barrier = pltpu.get_barrier_semaphore()

    def greet_seq(d, c):
        pl.semaphore_signal(barrier, inc=1, device_id={"seq": lax.rem(me + d, n)}, device_id_type=MESH)
        return c

    def greet_grp(d, c):
        pl.semaphore_signal(barrier, inc=1, device_id={"grp": lax.rem(g + d, m)}, device_id_type=MESH)
        return c

    lax.fori_loop(1, n, greet_seq, 0)
    lax.fori_loop(1, m, greet_grp, 0)

    def sums(h, c):
        cols = pl.ds(pl.multiple_of(h * HEAD_DIM, HEAD_DIM), HEAD_DIM)
        acc = None
        for b in range(count):
            r = pl.ds(b * BLOCK, BLOCK)
            key = silu(k_ref[r, cols])
            ks[r, cols] = key
            kv = lax.dot_general(key, v_ref[r, cols], (((0,), (0,)), ((), ())), preferred_element_type=F32)
            acc = kv if acc is None else acc + kv
            if b < count - 1:
                first[b, cols, :] = acc
        own[cols, :] = acc
        return c

    lax.fori_loop(0, HEADS, sums, 0)
    pl.semaphore_wait(barrier, n - 1 + m - 1)

    def scatter(j, sender):
        return pltpu.make_async_remote_copy(
            src_ref=own.at[rows_of(j)], dst_ref=gather.at[sender], send_sem=send1.at[j],
            recv_sem=recv1.at[sender], device_id={"seq": j}, device_id_type=MESH)

    def start1(d, c):
        scatter(lax.rem(me + d, n), me).start()
        return c

    lax.fori_loop(1, n, start1, 0)
    gather[me] = own[rows_of(me), :]

    causal = lax.broadcasted_iota(jnp.int32, (BLOCK, BLOCK), 0) >= lax.broadcasted_iota(jnp.int32, (BLOCK, BLOCK), 1)

    def inside(h, c):
        cols = pl.ds(pl.multiple_of(h * HEAD_DIM, HEAD_DIM), HEAD_DIM)
        for b in range(count):
            r = pl.ds(b * BLOCK, BLOCK)
            query = silu(q_ref[r, cols])
            qs[r, cols] = query
            scores = lax.dot_general(query, ks[r, cols], (((1,), (1,)), ((), ())), preferred_element_type=F32)
            scores = jnp.where(causal, scores, 0.0).astype(BF16)
            inner[r, cols] = jnp.dot(scores, v_ref[r, cols], preferred_element_type=F32)
        return c

    lax.fori_loop(0, HEADS, inside, 0)

    def wait1(d, c):
        scatter(me, lax.rem(me + d, n)).wait_recv()
        return c

    lax.fori_loop(1, n, wait1, 0)
    total[...] = lax.fori_loop(1, n, lambda s, t: t + gather[s], gather[0])

    def share(j, sender):
        return pltpu.make_async_remote_copy(
            src_ref=total, dst_ref=bases.at[sender], send_sem=send2.at[j],
            recv_sem=recv2.at[sender], device_id={"grp": j}, device_id_type=MESH)

    def start2(j, c):
        share(j, g).start()
        return c

    lax.fori_loop(g + 1, m, start2, 0)

    def wait2(j, t):
        share(g, j).wait_recv()
        return t + bases[j]

    base = lax.fori_loop(0, g, wait2, jnp.zeros((piece, HEAD_DIM), F32))

    def running(s, t):
        mine = gather[s]
        gather[s] = t
        return t + mine

    lax.fori_loop(0, n, running, base)

    def spread(j, sender):
        return pltpu.make_async_remote_copy(
            src_ref=gather.at[j], dst_ref=state.at[rows_of(sender)], send_sem=send3.at[j],
            recv_sem=recv3.at[sender], device_id={"seq": j}, device_id_type=MESH)

    def start3(d, c):
        j = lax.rem(me + d, n)
        spread(j, me).start()
        return c

    lax.fori_loop(1, n, start3, 0)
    state[rows_of(me), :] = gather[me]

    def finish(i, c):
        h = lax.rem(me // per_head + HEADS - i, HEADS)
        cols = pl.ds(pl.multiple_of(h * HEAD_DIM, HEAD_DIM), HEAD_DIM)

        def arrive(p, c):
            s = h * per_head + p

            @pl.when(s != me)
            def _():
                spread(me, s).wait_recv()
            return c

        lax.fori_loop(0, per_head, arrive, 0)
        before = state[cols, :]
        for b in range(count):
            r = pl.ds(b * BLOCK, BLOCK)
            now = before if b == 0 else before + first[b - 1, cols, :]
            high = now.astype(BF16)
            low = (now - high.astype(F32)).astype(BF16)
            query = qs[r, cols]
            mixed = inner[r, cols] + jnp.dot(
                jnp.concatenate([query, query], axis=1), jnp.concatenate([high, low], axis=0),
                preferred_element_type=F32)
            power = jnp.mean(mixed * mixed, axis=-1, keepdims=True)
            scale = gain_ref[0:1, cols] / (1.0 + jnp.exp(-gate_ref[r, cols].astype(F32)))
            out_ref[r, cols] = (mixed * lax.rsqrt(power + 1e-05) * scale).astype(BF16)
        return c

    lax.fori_loop(0, HEADS, finish, 0)

    def sent(d, c):
        j = lax.rem(me + d, n)
        scatter(j, me).wait_send()
        spread(j, me).wait_send()
        return c

    lax.fori_loop(1, n, sent, 0)

    def sent2(j, c):
        share(j, g).wait_send()
        return c

    lax.fori_loop(g + 1, m, sent2, 0)


def per_device(m, n, query, key_in, value, gate, gain):
    rows, features = query.shape
    count = rows // BLOCK
    piece = features // n
    whole = pl.BlockSpec(memory_space=pltpu.VMEM)
    dma = pltpu.SemaphoreType.DMA
    return pl.pallas_call(
        functools.partial(kernel, m, n),
        out_shape=jax.ShapeDtypeStruct((rows, features), BF16),
        in_specs=[whole] * 5,
        out_specs=whole,
        scratch_shapes=[
            pltpu.VMEM((rows, features), BF16),
            pltpu.VMEM((rows, features), BF16),
            pltpu.VMEM((features, HEAD_DIM), F32),
            pltpu.VMEM((max(count - 1, 1), features, HEAD_DIM), F32),
            pltpu.VMEM((n, piece, HEAD_DIM), F32),
            pltpu.VMEM((m, piece, HEAD_DIM), F32),
            pltpu.VMEM((piece, HEAD_DIM), F32),
            pltpu.VMEM((features, HEAD_DIM), F32),
            pltpu.VMEM((rows, features), F32),
            dma((n,)), dma((n,)), dma((m,)), dma((m,)), dma((n,)), dma((n,)),
        ],
        compiler_params=pltpu.CompilerParams(
            collective_id=0, has_side_effects=True, vmem_limit_bytes=40 * 1024 * 1024),
    )(query, key_in, value, gate, gain.reshape(1, features))


def solution(mesh):
    m, n = mesh.shape["grp"], mesh.shape["seq"]
    return jax.shard_map(
        functools.partial(per_device, m, n),
        mesh=mesh,
        in_specs=(
            P(("grp", "seq"), None),
            P(("grp", "seq"), None),
            P(("grp", "seq"), None),
            P(("grp", "seq"), None),
            P(),
        ),
        out_specs=P(("grp", "seq"), None),
        check_vma=False,
    )
```

```python
import functools

import jax
import jax.numpy as jnp
from jax import lax
from jax.experimental import pallas as pl
from jax.experimental.pallas import tpu as pltpu
from jax.sharding import PartitionSpec as P

HEADS = 8
HEAD_DIM = 128
BLOCK = 256
MESH = pl.DeviceIdType.MESH
F32 = jnp.float32
BF16 = jnp.bfloat16


def silu(u):
    u = u.astype(F32)
    return (u / (1.0 + jnp.exp(-u))).astype(BF16)


def kernel(m, n, q_hbm, k_hbm, v_hbm, gate_hbm, gain_ref, out_hbm, out_ref, q_ref, k_ref, v_ref, gate_ref, scale, ks, qs, own, first, gather, bases, total,
           state, inner, send1, recv1, send2, recv2, send3, recv3, k_sem, v_sem, q_sem, gate_sem, out_sem):
    g = lax.axis_index("grp")
    me = lax.axis_index("seq")
    rows = q_ref.shape[0]
    count = rows // BLOCK
    piece = HEADS * HEAD_DIM // n
    per_head = n // HEADS

    def rows_of(j):
        return pl.ds(pl.multiple_of(j * piece, piece), piece)

    barrier = pltpu.get_barrier_semaphore()

    def greet_seq(d, c):
        pl.semaphore_signal(barrier, inc=1, device_id={"seq": lax.rem(me + d, n)}, device_id_type=MESH)
        return c

    def greet_grp(d, c):
        pl.semaphore_signal(barrier, inc=1, device_id={"grp": lax.rem(g + d, m)}, device_id_type=MESH)
        return c

    lax.fori_loop(1, n, greet_seq, 0)
    lax.fori_loop(1, m, greet_grp, 0)

    def turn(i):
        return lax.rem(me // per_head + 1 + i, HEADS)

    def load(src, dst, sem, h):
        cols = pl.ds(pl.multiple_of(h * HEAD_DIM, HEAD_DIM), HEAD_DIM)
        return pltpu.make_async_copy(src.at[:, cols], dst.at[:, cols], sem.at[h])

    def loads(i, c):
        load(k_hbm, k_ref, k_sem, turn(i)).start()
        load(v_hbm, v_ref, v_sem, turn(i)).start()
        return c

    lax.fori_loop(0, HEADS, loads, 0)
    load_q = pltpu.make_async_copy(q_hbm, q_ref, q_sem)
    load_gate = pltpu.make_async_copy(gate_hbm, gate_ref, gate_sem)
    load_q.start()
    load_gate.start()
    pl.semaphore_wait(barrier, n - 1 + m - 1)

    def scatter(j, sender):
        return pltpu.make_async_remote_copy(
            src_ref=own.at[rows_of(j)], dst_ref=gather.at[sender], send_sem=send1.at[j],
            recv_sem=recv1.at[sender], device_id={"seq": j}, device_id_type=MESH)

    def sums(i, c):
        h = turn(i)
        cols = pl.ds(pl.multiple_of(h * HEAD_DIM, HEAD_DIM), HEAD_DIM)
        load(k_hbm, k_ref, k_sem, h).wait()
        load(v_hbm, v_ref, v_sem, h).wait()
        acc = None
        for b in range(count):
            r = pl.ds(b * BLOCK, BLOCK)
            key = silu(k_ref[r, cols])
            ks[r, cols] = key
            kv = lax.dot_general(key, v_ref[r, cols], (((0,), (0,)), ((), ())), preferred_element_type=F32)
            acc = kv if acc is None else acc + kv
            if b < count - 1:
                first[b, cols, :] = acc
        own[cols, :] = acc

        def send(p, c):
            j = h * per_head + p

            @pl.when(j != me)
            def _():
                scatter(j, me).start()
            return c

        lax.fori_loop(0, per_head, send, 0)
        return c

    lax.fori_loop(0, HEADS, sums, 0)
    gather[me] = own[rows_of(me), :]

    causal = lax.broadcasted_iota(jnp.int32, (BLOCK, BLOCK), 0) >= lax.broadcasted_iota(jnp.int32, (BLOCK, BLOCK), 1)

    def inside(h, c):
        cols = pl.ds(pl.multiple_of(h * HEAD_DIM, HEAD_DIM), HEAD_DIM)
        for b in range(count):
            r = pl.ds(b * BLOCK, BLOCK)
            query = silu(q_ref[r, cols])
            qs[r, cols] = query
            scores = lax.dot_general(query, ks[r, cols], (((1,), (1,)), ((), ())), preferred_element_type=F32)
            scores = jnp.where(causal, scores, 0.0).astype(BF16)
            inner[r, cols] = jnp.dot(scores, v_ref[r, cols], preferred_element_type=F32)
            scale[r, cols] = gain_ref[0:1, cols] / (1.0 + jnp.exp(-gate_ref[r, cols].astype(F32)))
        return c

    load_q.wait()
    load_gate.wait()
    lax.fori_loop(0, HEADS, inside, 0)

    def wait1(d, c):
        scatter(me, lax.rem(me + d, n)).wait_recv()
        return c

    lax.fori_loop(1, n, wait1, 0)
    total[...] = lax.fori_loop(1, n, lambda s, t: t + gather[s], gather[0])

    def share(j, sender):
        return pltpu.make_async_remote_copy(
            src_ref=total, dst_ref=bases.at[sender], send_sem=send2.at[j],
            recv_sem=recv2.at[sender], device_id={"grp": j}, device_id_type=MESH)

    def start2(j, c):
        share(j, g).start()
        return c

    lax.fori_loop(g + 1, m, start2, 0)

    def wait2(j, t):
        share(g, j).wait_recv()
        return t + bases[j]

    base = lax.fori_loop(0, g, wait2, jnp.zeros((piece, HEAD_DIM), F32))

    def running(s, t):
        mine = gather[s]
        gather[s] = t
        return t + mine

    lax.fori_loop(0, n, running, base)

    def spread(j, sender):
        return pltpu.make_async_remote_copy(
            src_ref=gather.at[j], dst_ref=state.at[rows_of(sender)], send_sem=send3.at[j],
            recv_sem=recv3.at[sender], device_id={"seq": j}, device_id_type=MESH)

    def start3(d, c):
        j = lax.rem(me + d, n)
        spread(j, me).start()
        return c

    lax.fori_loop(1, n, start3, 0)
    state[rows_of(me), :] = gather[me]

    def finish(i, c):
        h = lax.rem(me // per_head + HEADS - i, HEADS)
        cols = pl.ds(pl.multiple_of(h * HEAD_DIM, HEAD_DIM), HEAD_DIM)

        def arrive(p, c):
            s = h * per_head + p

            @pl.when(s != me)
            def _():
                spread(me, s).wait_recv()
            return c

        lax.fori_loop(0, per_head, arrive, 0)
        before = state[cols, :]
        for b in range(count):
            r = pl.ds(b * BLOCK, BLOCK)
            now = before if b == 0 else before + first[b - 1, cols, :]
            high = now.astype(BF16)
            low = (now - high.astype(F32)).astype(BF16)
            query = qs[r, cols]
            mixed = inner[r, cols] + jnp.dot(
                jnp.concatenate([query, query], axis=1), jnp.concatenate([high, low], axis=0),
                preferred_element_type=F32)
            power = jnp.mean(mixed * mixed, axis=-1, keepdims=True)
            out_ref[r, cols] = (mixed * lax.rsqrt(power + 1e-05) * scale[r, cols]).astype(BF16)
        load(out_ref, out_hbm, out_sem, h).start()
        return c

    lax.fori_loop(0, HEADS, finish, 0)

    def stored(h, c):
        load(out_ref, out_hbm, out_sem, h).wait()
        return c

    lax.fori_loop(0, HEADS, stored, 0)

    def sent(d, c):
        j = lax.rem(me + d, n)
        scatter(j, me).wait_send()
        spread(j, me).wait_send()
        return c

    lax.fori_loop(1, n, sent, 0)

    def sent2(j, c):
        share(j, g).wait_send()
        return c

    lax.fori_loop(g + 1, m, sent2, 0)


def per_device(m, n, query, key_in, value, gate, gain):
    rows, features = query.shape
    count = rows // BLOCK
    piece = features // n
    whole = pl.BlockSpec(memory_space=pltpu.VMEM)
    dma = pltpu.SemaphoreType.DMA
    return pl.pallas_call(
        functools.partial(kernel, m, n),
        out_shape=jax.ShapeDtypeStruct((rows, features), BF16),
        in_specs=[pl.BlockSpec(memory_space=pltpu.HBM)] * 4 + [whole],
        out_specs=pl.BlockSpec(memory_space=pltpu.HBM),
        scratch_shapes=[
            pltpu.VMEM((rows, features), BF16),
            pltpu.VMEM((rows, features), BF16),
            pltpu.VMEM((rows, features), BF16),
            pltpu.VMEM((rows, features), BF16),
            pltpu.VMEM((rows, features), BF16),
            pltpu.VMEM((rows, features), F32),
            pltpu.VMEM((rows, features), BF16),
            pltpu.VMEM((rows, features), BF16),
            pltpu.VMEM((features, HEAD_DIM), F32),
            pltpu.VMEM((max(count - 1, 1), features, HEAD_DIM), F32),
            pltpu.VMEM((n, piece, HEAD_DIM), F32),
            pltpu.VMEM((m, piece, HEAD_DIM), F32),
            pltpu.VMEM((piece, HEAD_DIM), F32),
            pltpu.VMEM((features, HEAD_DIM), F32),
            pltpu.VMEM((rows, features), F32),
            dma((n,)), dma((n,)), dma((m,)), dma((m,)), dma((n,)), dma((n,)),
            dma((HEADS,)), dma((HEADS,)), dma, dma, dma((HEADS,)),
        ],
        compiler_params=pltpu.CompilerParams(
            collective_id=0, has_side_effects=True, vmem_limit_bytes=62 * 1024 * 1024),
    )(query, key_in, value, gate, gain.reshape(1, features))


def solution(mesh):
    m, n = mesh.shape["grp"], mesh.shape["seq"]
    return jax.shard_map(
        functools.partial(per_device, m, n),
        mesh=mesh,
        in_specs=(
            P(("grp", "seq"), None),
            P(("grp", "seq"), None),
            P(("grp", "seq"), None),
            P(("grp", "seq"), None),
            P(),
        ),
        out_specs=P(("grp", "seq"), None),
        check_vma=False,
    )
```

```python
import functools

import jax
import jax.numpy as jnp
from jax import lax
from jax.experimental import pallas as pl
from jax.experimental.pallas import tpu as pltpu
from jax.sharding import PartitionSpec as P

HEADS = 8
HEAD_DIM = 128
BLOCK = 256
MESH = pl.DeviceIdType.MESH
F32 = jnp.float32
BF16 = jnp.bfloat16


def silu(u):
    u = u.astype(F32)
    return (u / (1.0 + jnp.exp(-u))).astype(BF16)


def kernel(m, n, q_hbm, k_hbm, v_hbm, gate_hbm, gain_ref, out_hbm, out_ref, q_ref, k_ref, v_ref, gate_ref, scale, ks, qs, own, first, gather, bases, total,
           state, inner, send1, recv1, send2, recv2, send3, recv3, k_sem, v_sem, q_sem, gate_sem, out_sem):
    g = lax.axis_index("grp")
    me = lax.axis_index("seq")
    rows = q_ref.shape[0]
    count = rows // BLOCK
    piece = HEADS * HEAD_DIM // n
    per_head = n // HEADS

    half = piece // 2

    def rows_of(j):
        return pl.ds(pl.multiple_of(j * piece, piece), piece)

    def half_of(j, part):
        return pl.ds(pl.multiple_of(j * piece + part * half, half), half)

    barrier = pltpu.get_barrier_semaphore()

    def greet_seq(d, c):
        pl.semaphore_signal(barrier, inc=1, device_id={"seq": lax.rem(me + d, n)}, device_id_type=MESH)
        return c

    def greet_grp(d, c):
        pl.semaphore_signal(barrier, inc=1, device_id={"grp": lax.rem(g + d, m)}, device_id_type=MESH)
        return c

    lax.fori_loop(1, n, greet_seq, 0)
    lax.fori_loop(1, m, greet_grp, 0)

    def turn(i):
        return lax.rem(me // per_head + 1 + i, HEADS)

    def load(src, dst, sem, h):
        cols = pl.ds(pl.multiple_of(h * HEAD_DIM, HEAD_DIM), HEAD_DIM)
        return pltpu.make_async_copy(src.at[:, cols], dst.at[:, cols], sem.at[h])

    def loads(i, c):
        load(k_hbm, k_ref, k_sem, turn(i)).start()
        load(v_hbm, v_ref, v_sem, turn(i)).start()
        return c

    lax.fori_loop(0, HEADS, loads, 0)
    load_q = pltpu.make_async_copy(q_hbm, q_ref, q_sem)
    load_gate = pltpu.make_async_copy(gate_hbm, gate_ref, gate_sem)
    load_q.start()
    load_gate.start()
    pl.semaphore_wait(barrier, n - 1 + m - 1)

    def scatter(j, sender, part):
        return pltpu.make_async_remote_copy(
            src_ref=own.at[half_of(j, part)], dst_ref=gather.at[sender, half_of(0, part)],
            send_sem=send1.at[part, j], recv_sem=recv1.at[part, sender], device_id={"seq": j}, device_id_type=MESH)

    def sums(i, c):
        h = turn(i)
        cols = pl.ds(pl.multiple_of(h * HEAD_DIM, HEAD_DIM), HEAD_DIM)
        load(k_hbm, k_ref, k_sem, h).wait()
        load(v_hbm, v_ref, v_sem, h).wait()
        acc = None
        for b in range(count):
            r = pl.ds(b * BLOCK, BLOCK)
            key = silu(k_ref[r, cols])
            ks[r, cols] = key
            kv = lax.dot_general(key, v_ref[r, cols], (((0,), (0,)), ((), ())), preferred_element_type=F32)
            acc = kv if acc is None else acc + kv
            if b < count - 1:
                first[b, cols, :] = acc
        own[cols, :] = acc

        def send(p, c):
            j = h * per_head + p

            @pl.when(j != me)
            def _():
                scatter(j, me, 0).start()
            return c

        lax.fori_loop(0, per_head, send, 0)
        return c

    lax.fori_loop(0, HEADS, sums, 0)

    def start1(d, c):
        scatter(lax.rem(me + d, n), me, 1).start()
        return c

    lax.fori_loop(1, n, start1, 0)
    gather[me] = own[rows_of(me), :]

    causal = lax.broadcasted_iota(jnp.int32, (BLOCK, BLOCK), 0) >= lax.broadcasted_iota(jnp.int32, (BLOCK, BLOCK), 1)

    def inside(h, c):
        cols = pl.ds(pl.multiple_of(h * HEAD_DIM, HEAD_DIM), HEAD_DIM)
        for b in range(count):
            r = pl.ds(b * BLOCK, BLOCK)
            query = silu(q_ref[r, cols])
            qs[r, cols] = query
            scores = lax.dot_general(query, ks[r, cols], (((1,), (1,)), ((), ())), preferred_element_type=F32)
            scores = jnp.where(causal, scores, 0.0).astype(BF16)
            inner[r, cols] = jnp.dot(scores, v_ref[r, cols], preferred_element_type=F32)
            scale[r, cols] = gain_ref[0:1, cols] / (1.0 + jnp.exp(-gate_ref[r, cols].astype(F32)))
        return c

    load_q.wait()
    load_gate.wait()
    lax.fori_loop(0, HEADS, inside, 0)

    def share(j, sender, part):
        return pltpu.make_async_remote_copy(
            src_ref=total.at[half_of(0, part)], dst_ref=bases.at[sender, half_of(0, part)],
            send_sem=send2.at[part, j], recv_sem=recv2.at[part, sender], device_id={"grp": j}, device_id_type=MESH)

    def spread(j, sender, part):
        return pltpu.make_async_remote_copy(
            src_ref=gather.at[j, half_of(0, part)], dst_ref=state.at[half_of(sender, part)],
            send_sem=send3.at[part, j], recv_sem=recv3.at[part, sender], device_id={"seq": j}, device_id_type=MESH)

    for part in range(2):
        here = half_of(0, part)

        def wait1(d, c):
            scatter(me, lax.rem(me + d, n), part).wait_recv()
            return c

        lax.fori_loop(1, n, wait1, 0)
        total[here, :] = lax.fori_loop(1, n, lambda s, t: t + gather[s, here, :], gather[0, here, :])

        def start2(j, c):
            share(j, g, part).start()
            return c

        lax.fori_loop(g + 1, m, start2, 0)

    for part in range(2):
        here = half_of(0, part)

        def wait2(j, t):
            share(g, j, part).wait_recv()
            return t + bases[j, here, :]

        base = lax.fori_loop(0, g, wait2, jnp.zeros((half, HEAD_DIM), F32))

        def running(s, t):
            mine = gather[s, here, :]
            gather[s, here, :] = t
            return t + mine

        lax.fori_loop(0, n, running, base)

        def start3(d, c):
            spread(lax.rem(me + d, n), me, part).start()
            return c

        lax.fori_loop(1, n, start3, 0)

    state[rows_of(me), :] = gather[me]

    def finish(i, c):
        h = lax.rem(me // per_head + HEADS - i, HEADS)
        cols = pl.ds(pl.multiple_of(h * HEAD_DIM, HEAD_DIM), HEAD_DIM)

        def arrive(p, c):
            s = h * per_head + p

            @pl.when(s != me)
            def _():
                spread(me, s, 0).wait_recv()
                spread(me, s, 1).wait_recv()
            return c

        lax.fori_loop(0, per_head, arrive, 0)
        before = state[cols, :]
        for b in range(count):
            r = pl.ds(b * BLOCK, BLOCK)
            now = before if b == 0 else before + first[b - 1, cols, :]
            high = now.astype(BF16)
            low = (now - high.astype(F32)).astype(BF16)
            query = qs[r, cols]
            mixed = inner[r, cols] + jnp.dot(
                jnp.concatenate([query, query], axis=1), jnp.concatenate([high, low], axis=0),
                preferred_element_type=F32)
            power = jnp.mean(mixed * mixed, axis=-1, keepdims=True)
            out_ref[r, cols] = (mixed * lax.rsqrt(power + 1e-05) * scale[r, cols]).astype(BF16)
        load(out_ref, out_hbm, out_sem, h).start()
        return c

    lax.fori_loop(0, HEADS, finish, 0)

    def stored(h, c):
        load(out_ref, out_hbm, out_sem, h).wait()
        return c

    lax.fori_loop(0, HEADS, stored, 0)

    def sent(d, c):
        j = lax.rem(me + d, n)
        for part in range(2):
            scatter(j, me, part).wait_send()
            spread(j, me, part).wait_send()
        return c

    lax.fori_loop(1, n, sent, 0)

    def sent2(j, c):
        share(j, g, 0).wait_send()
        share(j, g, 1).wait_send()
        return c

    lax.fori_loop(g + 1, m, sent2, 0)


def per_device(m, n, query, key_in, value, gate, gain):
    rows, features = query.shape
    count = rows // BLOCK
    piece = features // n
    whole = pl.BlockSpec(memory_space=pltpu.VMEM)
    dma = pltpu.SemaphoreType.DMA
    return pl.pallas_call(
        functools.partial(kernel, m, n),
        out_shape=jax.ShapeDtypeStruct((rows, features), BF16),
        in_specs=[pl.BlockSpec(memory_space=pltpu.HBM)] * 4 + [whole],
        out_specs=pl.BlockSpec(memory_space=pltpu.HBM),
        scratch_shapes=[
            pltpu.VMEM((rows, features), BF16),
            pltpu.VMEM((rows, features), BF16),
            pltpu.VMEM((rows, features), BF16),
            pltpu.VMEM((rows, features), BF16),
            pltpu.VMEM((rows, features), BF16),
            pltpu.VMEM((rows, features), F32),
            pltpu.VMEM((rows, features), BF16),
            pltpu.VMEM((rows, features), BF16),
            pltpu.VMEM((features, HEAD_DIM), F32),
            pltpu.VMEM((max(count - 1, 1), features, HEAD_DIM), F32),
            pltpu.VMEM((n, piece, HEAD_DIM), F32),
            pltpu.VMEM((m, piece, HEAD_DIM), F32),
            pltpu.VMEM((piece, HEAD_DIM), F32),
            pltpu.VMEM((features, HEAD_DIM), F32),
            pltpu.VMEM((rows, features), F32),
            dma((2, n)), dma((2, n)), dma((2, m)), dma((2, m)), dma((2, n)), dma((2, n)),
            dma((HEADS,)), dma((HEADS,)), dma, dma, dma((HEADS,)),
        ],
        compiler_params=pltpu.CompilerParams(
            collective_id=0, has_side_effects=True, vmem_limit_bytes=62 * 1024 * 1024),
    )(query, key_in, value, gate, gain.reshape(1, features))


def solution(mesh):
    m, n = mesh.shape["grp"], mesh.shape["seq"]
    return jax.shard_map(
        functools.partial(per_device, m, n),
        mesh=mesh,
        in_specs=(
            P(("grp", "seq"), None),
            P(("grp", "seq"), None),
            P(("grp", "seq"), None),
            P(("grp", "seq"), None),
            P(),
        ),
        out_specs=P(("grp", "seq"), None),
        check_vma=False,
    )
```

```python
import functools

import jax
import jax.numpy as jnp
from jax import lax
from jax.experimental import pallas as pl
from jax.experimental.pallas import tpu as pltpu
from jax.sharding import PartitionSpec as P

HEADS = 8
HEAD_DIM = 128
BLOCK = 256
MESH = pl.DeviceIdType.MESH
F32 = jnp.float32
BF16 = jnp.bfloat16


def silu(u):
    u = u.astype(F32)
    return (u / (1.0 + jnp.exp(-u))).astype(BF16)


def kernel(m, n, q_hbm, k_hbm, v_hbm, gate_hbm, gain_ref, out_hbm, out_ref, q_ref, k_ref, v_ref, gate_ref, scale, ks, qs, own, first, gather, bases, total,
           state, inner, send1, recv1, send2, recv2, send3, recv3, k_sem, v_sem, q_sem, gate_sem, out_sem):
    g = lax.axis_index("grp")
    me = lax.axis_index("seq")
    rows = q_ref.shape[0]
    count = rows // BLOCK
    piece = HEADS * HEAD_DIM // n
    per_head = n // HEADS

    half = piece // 2

    def rows_of(j):
        return pl.ds(pl.multiple_of(j * piece, piece), piece)

    def half_of(j, part):
        return pl.ds(pl.multiple_of(j * piece + part * half, half), half)

    barrier = pltpu.get_barrier_semaphore()

    def greet_seq(d, c):
        pl.semaphore_signal(barrier, inc=1, device_id={"seq": lax.rem(me + d, n)}, device_id_type=MESH)
        return c

    def greet_grp(d, c):
        pl.semaphore_signal(barrier, inc=1, device_id={"grp": lax.rem(g + d, m)}, device_id_type=MESH)
        return c

    lax.fori_loop(1, n, greet_seq, 0)
    lax.fori_loop(1, m, greet_grp, 0)

    def turn(i):
        return lax.rem(me // per_head + 1 + i, HEADS)

    def load(src, dst, sem, h):
        cols = pl.ds(pl.multiple_of(h * HEAD_DIM, HEAD_DIM), HEAD_DIM)
        return pltpu.make_async_copy(src.at[:, cols], dst.at[:, cols], sem.at[h])

    def loads(i, c):
        load(k_hbm, k_ref, k_sem, turn(i)).start()
        load(v_hbm, v_ref, v_sem, turn(i)).start()
        return c

    lax.fori_loop(0, HEADS, loads, 0)
    load_q = pltpu.make_async_copy(q_hbm, q_ref, q_sem)
    load_gate = pltpu.make_async_copy(gate_hbm, gate_ref, gate_sem)
    load_q.start()
    load_gate.start()

    def scatter(j, sender, part):
        return pltpu.make_async_remote_copy(
            src_ref=own.at[half_of(j, part)], dst_ref=gather.at[sender, half_of(0, part)],
            send_sem=send1.at[part, j], recv_sem=recv1.at[part, sender], device_id={"seq": j}, device_id_type=MESH)

    def sums(i, c):
        h = turn(i)
        cols = pl.ds(pl.multiple_of(h * HEAD_DIM, HEAD_DIM), HEAD_DIM)
        load(k_hbm, k_ref, k_sem, h).wait()
        load(v_hbm, v_ref, v_sem, h).wait()
        acc = None
        for b in range(count):
            r = pl.ds(b * BLOCK, BLOCK)
            key = silu(k_ref[r, cols])
            ks[r, cols] = key
            kv = lax.dot_general(key, v_ref[r, cols], (((0,), (0,)), ((), ())), preferred_element_type=F32)
            acc = kv if acc is None else acc + kv
            if b < count - 1:
                first[b, cols, :] = acc
        own[cols, :] = acc
        return c

    def post(i, c):
        h = turn(i)

        def send(p, c):
            j = h * per_head + p

            @pl.when(j != me)
            def _():
                scatter(j, me, 0).start()
            return c

        lax.fori_loop(0, per_head, send, 0)
        return c

    sums(0, 0)
    pl.semaphore_wait(barrier, n - 1 + m - 1)
    post(0, 0)
    lax.fori_loop(1, HEADS, lambda i, c: post(i, sums(i, c)), 0)

    def start1(d, c):
        scatter(lax.rem(me + d, n), me, 1).start()
        return c

    lax.fori_loop(1, n, start1, 0)
    gather[me] = own[rows_of(me), :]

    causal = lax.broadcasted_iota(jnp.int32, (BLOCK, BLOCK), 0) >= lax.broadcasted_iota(jnp.int32, (BLOCK, BLOCK), 1)

    def inside(h, c):
        cols = pl.ds(pl.multiple_of(h * HEAD_DIM, HEAD_DIM), HEAD_DIM)
        for b in range(count):
            r = pl.ds(b * BLOCK, BLOCK)
            query = silu(q_ref[r, cols])
            qs[r, cols] = query
            scores = lax.dot_general(query, ks[r, cols], (((1,), (1,)), ((), ())), preferred_element_type=F32)
            scores = jnp.where(causal, scores, 0.0).astype(BF16)
            inner[r, cols] = jnp.dot(scores, v_ref[r, cols], preferred_element_type=F32)
            scale[r, cols] = gain_ref[0:1, cols] / (1.0 + jnp.exp(-gate_ref[r, cols].astype(F32)))
        return c

    load_q.wait()
    load_gate.wait()
    lax.fori_loop(0, HEADS, inside, 0)

    def share(j, sender, part):
        return pltpu.make_async_remote_copy(
            src_ref=total.at[half_of(0, part)], dst_ref=bases.at[sender, half_of(0, part)],
            send_sem=send2.at[part, j], recv_sem=recv2.at[part, sender], device_id={"grp": j}, device_id_type=MESH)

    def spread(j, sender, part):
        return pltpu.make_async_remote_copy(
            src_ref=gather.at[j, half_of(0, part)], dst_ref=state.at[half_of(sender, part)],
            send_sem=send3.at[part, j], recv_sem=recv3.at[part, sender], device_id={"seq": j}, device_id_type=MESH)

    for part in range(2):
        here = half_of(0, part)

        def wait1(d, c):
            scatter(me, lax.rem(me + d, n), part).wait_recv()
            return c

        lax.fori_loop(1, n, wait1, 0)
        total[here, :] = lax.fori_loop(1, n, lambda s, t: t + gather[s, here, :], gather[0, here, :])

        def start2(j, c):
            share(j, g, part).start()
            return c

        lax.fori_loop(g + 1, m, start2, 0)

    for part in range(2):
        here = half_of(0, part)

        def wait2(j, t):
            share(g, j, part).wait_recv()
            return t + bases[j, here, :]

        base = lax.fori_loop(0, g, wait2, jnp.zeros((half, HEAD_DIM), F32))

        def running(s, t):
            mine = gather[s, here, :]
            gather[s, here, :] = t
            return t + mine

        lax.fori_loop(0, n, running, base)

        def start3(d, c):
            spread(lax.rem(me + d, n), me, part).start()
            return c

        lax.fori_loop(1, n, start3, 0)

    state[rows_of(me), :] = gather[me]

    def finish(i, c):
        h = lax.rem(me // per_head + HEADS - i, HEADS)
        cols = pl.ds(pl.multiple_of(h * HEAD_DIM, HEAD_DIM), HEAD_DIM)

        def arrive(p, c):
            s = h * per_head + p

            @pl.when(s != me)
            def _():
                spread(me, s, 0).wait_recv()
                spread(me, s, 1).wait_recv()
            return c

        lax.fori_loop(0, per_head, arrive, 0)
        before = state[cols, :]
        for b in range(count):
            r = pl.ds(b * BLOCK, BLOCK)
            now = before if b == 0 else before + first[b - 1, cols, :]
            high = now.astype(BF16)
            low = (now - high.astype(F32)).astype(BF16)
            query = qs[r, cols]
            mixed = inner[r, cols] + jnp.dot(
                jnp.concatenate([query, query], axis=1), jnp.concatenate([high, low], axis=0),
                preferred_element_type=F32)
            power = jnp.mean(mixed * mixed, axis=-1, keepdims=True)
            out_ref[r, cols] = (mixed * lax.rsqrt(power + 1e-05) * scale[r, cols]).astype(BF16)
        load(out_ref, out_hbm, out_sem, h).start()
        return c

    lax.fori_loop(0, HEADS, finish, 0)

    def stored(h, c):
        load(out_ref, out_hbm, out_sem, h).wait()
        return c

    lax.fori_loop(0, HEADS, stored, 0)

    def sent(d, c):
        j = lax.rem(me + d, n)
        for part in range(2):
            scatter(j, me, part).wait_send()
            spread(j, me, part).wait_send()
        return c

    lax.fori_loop(1, n, sent, 0)

    def sent2(j, c):
        share(j, g, 0).wait_send()
        share(j, g, 1).wait_send()
        return c

    lax.fori_loop(g + 1, m, sent2, 0)


def per_device(m, n, query, key_in, value, gate, gain):
    rows, features = query.shape
    count = rows // BLOCK
    piece = features // n
    whole = pl.BlockSpec(memory_space=pltpu.VMEM)
    dma = pltpu.SemaphoreType.DMA
    return pl.pallas_call(
        functools.partial(kernel, m, n),
        out_shape=jax.ShapeDtypeStruct((rows, features), BF16),
        in_specs=[pl.BlockSpec(memory_space=pltpu.HBM)] * 4 + [whole],
        out_specs=pl.BlockSpec(memory_space=pltpu.HBM),
        scratch_shapes=[
            pltpu.VMEM((rows, features), BF16),
            pltpu.VMEM((rows, features), BF16),
            pltpu.VMEM((rows, features), BF16),
            pltpu.VMEM((rows, features), BF16),
            pltpu.VMEM((rows, features), BF16),
            pltpu.VMEM((rows, features), F32),
            pltpu.VMEM((rows, features), BF16),
            pltpu.VMEM((rows, features), BF16),
            pltpu.VMEM((features, HEAD_DIM), F32),
            pltpu.VMEM((max(count - 1, 1), features, HEAD_DIM), F32),
            pltpu.VMEM((n, piece, HEAD_DIM), F32),
            pltpu.VMEM((m, piece, HEAD_DIM), F32),
            pltpu.VMEM((piece, HEAD_DIM), F32),
            pltpu.VMEM((features, HEAD_DIM), F32),
            pltpu.VMEM((rows, features), F32),
            dma((2, n)), dma((2, n)), dma((2, m)), dma((2, m)), dma((2, n)), dma((2, n)),
            dma((HEADS,)), dma((HEADS,)), dma, dma, dma((HEADS,)),
        ],
        compiler_params=pltpu.CompilerParams(
            collective_id=0, has_side_effects=True, vmem_limit_bytes=62 * 1024 * 1024),
    )(query, key_in, value, gate, gain.reshape(1, features))


def solution(mesh):
    m, n = mesh.shape["grp"], mesh.shape["seq"]
    return jax.shard_map(
        functools.partial(per_device, m, n),
        mesh=mesh,
        in_specs=(
            P(("grp", "seq"), None),
            P(("grp", "seq"), None),
            P(("grp", "seq"), None),
            P(("grp", "seq"), None),
            P(),
        ),
        out_specs=P(("grp", "seq"), None),
        check_vma=False,
    )
```
